32 devices in a mesh: member: 2 (over x), grid: 16 (over z, y, core).
Axes of the slice: x: 2, y: 2, z: 4, core: 2. Of those that a mesh axis runs over, the one named last changes fastest.
Arguments:
- latent: bfloat16 [16, 49152, 512], P('member', 'grid'), may hold values from -6 to 6
- weight_in: bfloat16 [512, 512], replicated, may hold values from -0.25 to 0.25
- bias_in: float32 [512], replicated, may hold values from -3 to 3
- weight_out: bfloat16 [512, 8], replicated, may hold values from -0.25 to 0.25
- bias_out: float32 [8], replicated, may hold values from -3 to 3
- member_rank: int32 [16, 8, 49152], P('member', None, 'grid'), may hold values from 0 to 31, as said below
- target_level: int32 [8, 49152], P(None, 'grid'), may hold values from 0 to 32
- target_jitter: float32 [8, 49152], P(None, 'grid'), may hold values from -1 to 1
- var_weight: float32 [8], replicated, may hold values from 0.25 to 4
Outputs:
- grad_weight_in: float32 [512, 512], P('grid')
- grad_bias_in: float32 [512], replicated
- grad_weight_out: float32 [512, 8], replicated
- grad_bias_out: float32 [8], replicated
The draws below stay inside these ranges and needn't reach their ends.
Inputs may be any that keep to these rules, and one draw needn't show every extreme that they name: `member_rank`: at each variable and cell the 16 members' offsets are distinct whole numbers.
All inputs are finite; a program needn't handle non-finite values.
Results may differ from the reference program's by a relative error of at most 0.00069.
Values sent between devices are 32-bit elements; how exact they have to be, the bound alone decides.
A program may use at most 384 MiB of HBM per device.

```python
import math
import jax
import jax.numpy as jnp
from jax import lax

M = 16
D = 512
H = 512
VARS = 8
LONS = 1440
CELLS_DEV = 3072
CELLS = 49152
N_GRID = 16


def draw_member_rank(key, part):
    key = jax.random.fold_in(key, 3)
    base = jnp.broadcast_to(jnp.arange(2 * M, dtype=jnp.int32)[:, None, None], (2 * M, VARS, CELLS))
    shuffled = jax.random.permutation(key, base, axis=0, independent=True)
    return shuffled[:M]


def plant(values, stream_key, smallest, high):
    extent = values.shape
    place = [jax.random.randint(jax.random.fold_in(stream_key, axis), (), 0, extent[axis]) for axis in range(len(extent))]
    values = values.at[tuple(place)].set(smallest)
    longest = extent.index(max(extent))
    place[longest] = (place[longest] + 1) % extent[longest]
    return values.at[tuple(place)].set(high)


def strengthened(entries, rng, source, target, blocks, factor):
    def block_of(dim):
        return (jnp.arange(entries.shape[dim]) // (entries.shape[dim] // blocks)).reshape((-1,) + (1,) * (entries.ndim - 1 - dim))

    one_side = jax.random.permutation(rng, blocks)[block_of(target)]
    far = (block_of(target) + blocks // 2) % blocks
    return jnp.where((block_of(source) == one_side) | (block_of(source) == far), factor * entries, entries)


def block_scale(rng, dims, pieces, least, top_value):
    gain = 1.0
    for dim, parts in pieces:
        draws = jax.random.uniform(jax.random.fold_in(jax.random.fold_in(rng, 6), dim), (parts,), jnp.float32, least / len(pieces), top_value / len(pieces))
        gain = gain * jnp.repeat(jnp.exp(draws), dims[dim] // parts).reshape((-1,) + (1,) * (len(dims) - 1 - dim))
    return gain


def noise(own_key, shape, spread, most, shards=(), held_as=jnp.bfloat16):
    drawn = spread * jax.random.normal(own_key, shape, jnp.float32)
    if shards:
        drawn = drawn * block_scale(own_key, shape, shards, -0.22, 0.18)
    return jnp.clip(drawn, -most, most).astype(held_as)


def noise_with(own_key, shape, width, most, cuts, heavy, held_as=jnp.bfloat16):
    values = width * jax.random.normal(own_key, shape, jnp.float32)
    if cuts:
        values = values * block_scale(own_key, shape, cuts, -0.22, 0.18)
    return jnp.clip(strengthened(values, jax.random.fold_in(own_key, 3), *heavy), -most, most).astype(held_as)


def setup_inputs(seed: int = 0) -> dict:
    seeds = jax.random.split(jax.random.key(seed), 10)
    return {
        "latent": noise_with(seeds[0], (M, CELLS, D), 1.0, 6.0, ((0, 2), (1, 16)), (1, 2, 16, 2.0)),
        "weight_in": noise(seeds[1], (D, H), D ** -0.5, 0.25),
        "bias_in": noise(seeds[2], (H,), 0.5, 3.0, (), jnp.float32),
        "weight_out": noise(seeds[3], (H, VARS), H ** -0.5, 0.25),
        "bias_out": noise(seeds[4], (VARS,), 0.5, 3.0, (), jnp.float32),
        "member_rank": draw_member_rank(jax.random.fold_in(seeds[9], 71), 0),
        "target_level": plant(jax.random.randint(seeds[6], (VARS, CELLS), 0, 2 * M + 1), jax.random.fold_in(seeds[6], 1), 0, 2 * M).astype(jnp.int32),
        "target_jitter": jnp.clip(jax.random.uniform(seeds[7], (VARS, CELLS), jnp.float32, -1.0, 1.0) * block_scale(seeds[7], (VARS, CELLS), ((1, 16),), -0.4, 0.0), -1.0, 1.0),
        "var_weight": jnp.clip(jnp.exp(jax.random.uniform(seeds[8], (VARS,), jnp.float32, math.log(0.25), math.log(4.0))), 0.25, 4.0),
    }


north_row = 200.0
mean_weight = 0.05
smooth_square = 0.01

def area_weights(first_cell, count):
    global_cell = first_cell + jnp.arange(count, dtype=jnp.int32)
    lat_row = (global_cell // LONS).astype(jnp.float32)
    latitude = (90.0 - 0.25 * (north_row + lat_row)) * (math.pi / 180.0)
    return jnp.cos(latitude)

def soft_sign(values):
    return values / jnp.sqrt(values * values + smooth_square)

def crps_slopes(fields, target, area, var_weight):
    members = fields.shape[0]
    center = lax.optimization_barrier(jnp.mean(fields, axis=0))
    pair_sum = lax.optimization_barrier(jnp.sum(soft_sign(fields[:, None] - fields[None, :]), axis=1))
    weights = var_weight[:, None] * area[None, :]
    return weights[None] * (soft_sign(fields - target[None]) - pair_sum / (members - 1) + 2.0 * mean_weight * (center - target)[None])

def gelu_tanh(values):
    return jax.nn.gelu(values, approximate=True)

def block_grads(block_latent, weight_in, bias_in, weight_out, bias_out, rank_block, level_block, jitter_block, var_weight, first_cell, loss_scale):
    members, cell_count, in_width = block_latent.shape
    flat_rows = block_latent.reshape(members * cell_count, in_width)
    preact = jnp.dot(flat_rows, weight_in, preferred_element_type=jnp.float32) + bias_in
    hidden = gelu_tanh(preact).astype(jnp.bfloat16)
    hidden_cube = hidden.reshape(members, cell_count, -1)
    outputs = jnp.einsum('mch,hv->mvc', hidden_cube.astype(jnp.float32), weight_out.astype(jnp.float32)) + bias_out[None, :, None]
    squash = jnp.tanh(outputs)
    fields = 0.1 * rank_block.astype(jnp.float32) + squash
    target = 0.1 * level_block.astype(jnp.float32) + 0.5 * jitter_block - 0.5
    area = area_weights(first_cell, cell_count)
    slopes = crps_slopes(fields, target, area, var_weight)
    out_grad = slopes * (1.0 - squash * squash) * loss_scale
    out_grad_b = out_grad.astype(jnp.bfloat16)
    hid_grad = jnp.einsum('mvc,hv->mch', out_grad_b.astype(jnp.float32), weight_out.astype(jnp.float32)).reshape(members * cell_count, -1)
    gelu_out, pull_back = jax.vjp(gelu_tanh, preact)
    pre_grad = pull_back(hid_grad)[0]
    pre_grad_b = pre_grad.astype(jnp.bfloat16)
    grad_w_in = jnp.dot(flat_rows.T, pre_grad_b, preferred_element_type=jnp.float32)
    grad_b_in = lax.optimization_barrier(jnp.sum(pre_grad, axis=0))
    grad_w_out = jnp.einsum('mch,mvc->hv', hidden_cube.astype(jnp.float32), out_grad_b.astype(jnp.float32))
    grad_b_out = lax.optimization_barrier(jnp.sum(out_grad, axis=(0, 2)))
    return (grad_w_in, grad_b_in, grad_w_out, grad_b_out)

def reference(latent, weight_in, bias_in, weight_out, bias_out, member_rank, target_level, target_jitter, var_weight):
    all_cells = CELLS_DEV * N_GRID
    loss_scale = 2.0 / math.sqrt(all_cells * M)

    def step(block, totals):
        first_cell = jnp.asarray(block).astype(jnp.int32) * CELLS_DEV
        block_latent = lax.dynamic_slice_in_dim(latent, first_cell, CELLS_DEV, 1)
        rank_block = lax.dynamic_slice_in_dim(member_rank, first_cell, CELLS_DEV, 2)
        level_block = lax.dynamic_slice_in_dim(target_level, first_cell, CELLS_DEV, 1)
        jitter_block = lax.dynamic_slice_in_dim(target_jitter, first_cell, CELLS_DEV, 1)
        grads = block_grads(block_latent, weight_in, bias_in, weight_out, bias_out, rank_block, level_block, jitter_block, var_weight, first_cell, loss_scale)
        return tuple((left + right for left, right in zip(totals, grads)))
    init = (jnp.zeros((D, H), jnp.float32), jnp.zeros((H,), jnp.float32), jnp.zeros((H, VARS), jnp.float32), jnp.zeros((VARS,), jnp.float32))
    grad_w_in, grad_b_in, grad_w_out, grad_b_out = lax.fori_loop(0, N_GRID, step, init)
    return (grad_w_in, grad_b_in, grad_w_out, grad_b_out)
```

```python
import functools
import math

import jax
import jax.numpy as jnp
from jax import lax
from jax.experimental import pallas as pl
from jax.experimental.pallas import tpu as pltpu
from jax.sharding import PartitionSpec as P

LONS = 1440
LAG = 2
TILE = 128
CHUNK_ROWS = 256
SUB_ROWS = 32

north_row = 200.0
mean_weight = 0.05
smooth_square = 0.01
root_two_pi = math.sqrt(2.0 / math.pi)
cube_coef = 0.044715


def area_weights(first_cell, count):
    global_cell = first_cell + jnp.arange(count, dtype=jnp.int32)
    lat_row = (global_cell // LONS).astype(jnp.float32)
    latitude = (90.0 - 0.25 * (north_row + lat_row)) * (math.pi / 180.0)
    return jnp.cos(latitude)


def soft_sign(values):
    return values * lax.rsqrt(values * values + smooth_square)


def fused_kernel(
    groups,
    tiles,
    lat_ref,
    late_ref,
    w_in_ref,
    b_in_ref,
    w_out_t_ref,
    b_out_ref,
    rank_ref,
    level_ref,
    jitter_ref,
    weight_ref,
    grad_ref,
    small_ref,
    hid_buf,
    slope_buf,
    pre_buf,
    field_buf,
    squash_buf,
    recv_buf,
    bias_acc,
    out_acc,
    send_sem,
    recv_sem,
):
    step = pl.program_id(0)
    me = lax.axis_index("member")
    mem_dev, tile, in_width = lat_ref.shape
    width = w_in_ref.shape[1]
    nvars = w_out_t_ref.shape[0]
    rows = mem_dev * tile
    members = mem_dev * groups
    mem_chunk = max(1, CHUNK_ROWS // tile)
    chunk_rows = mem_chunk * tile

    def copies(index):
        made = []
        for hop in range(1, groups):
            made.append(
                pltpu.make_async_remote_copy(
                    src_ref=field_buf.at[index],
                    dst_ref=recv_buf.at[hop - 1, index],
                    send_sem=send_sem.at[hop - 1, index],
                    recv_sem=recv_sem.at[hop - 1, index],
                    device_id={"member": lax.rem(me + hop, groups)},
                    device_id_type=pl.DeviceIdType.MESH,
                )
            )
        return made

    def loss_part(index):
        own = [field_buf[index, pl.ds(m * nvars, nvars), :] for m in range(mem_dev)]
        other = [
            recv_buf[g, index, pl.ds(m * nvars, nvars), :]
            for g in range(groups - 1)
            for m in range(mem_dev)
        ]
        target = 0.1 * level_ref[...].astype(jnp.float32) + 0.5 * jitter_ref[...] - 0.5
        center = own[0]
        for value in own[1:] + other:
            center = center + value
        pull = (2.0 * mean_weight) * (center * (1.0 / members) - target)
        weight = weight_ref[...]
        pair = [jnp.zeros_like(target) for _ in range(mem_dev)]
        for a in range(mem_dev):
            for b in range(a + 1, mem_dev):
                value = soft_sign(own[a] - own[b])
                pair[a] = pair[a] + value
                pair[b] = pair[b] - value
            for value in other:
                pair[a] = pair[a] + soft_sign(own[a] - value)
        grads = []
        for m in range(mem_dev):
            squash = squash_buf[index, pl.ds(m * nvars, nvars), :]
            slope = weight * (soft_sign(own[m] - target) - pair[m] * (1.0 / (members - 1)) + pull)
            grads.append(slope * (1.0 - squash * squash))
        total = grads[0]
        for value in grads[1:]:
            total = total + value
        out_acc[...] += total
        return jnp.concatenate(grads, axis=1)

    def forward_chunk(index, slot, chunk):
        first = chunk * mem_chunk
        block = lat_ref[pl.ds(first, mem_chunk)].reshape(chunk_rows, in_width)
        raw = jnp.dot(block, w_in_ref[...], preferred_element_type=jnp.float32)
        bias = b_in_ref[...]
        for sub in range(0, chunk_rows, SUB_ROWS):
            pre = raw[sub : sub + SUB_ROWS] + bias
            square = pre * pre
            arg = pre * (root_two_pi + (root_two_pi * cube_coef) * square)
            gate = 0.5 + 0.5 * jnp.tanh(arg)
            hid = pre * gate
            rate = (2.0 * root_two_pi) + (6.0 * root_two_pi * cube_coef) * square
            place = pl.ds(chunk * chunk_rows + sub, SUB_ROWS)
            hid_buf[slot, place, :] = hid.astype(jnp.bfloat16)
            slope_buf[slot, place, :] = gate + hid * (1.0 - gate) * rate
        hid_block = hid_buf[slot, pl.ds(chunk * chunk_rows, chunk_rows), :]
        outs = lax.dot_general(
            w_out_t_ref[...], hid_block, (((1,), (1,)), ((), ())), preferred_element_type=jnp.float32
        )
        squash = jnp.tanh(outs + b_out_ref[...])
        for m in range(mem_chunk):
            part = squash[:, m * tile : (m + 1) * tile]
            place = pl.ds((first + m) * nvars, nvars)
            squash_buf[index, place, :] = part
            field_buf[index, place, :] = 0.1 * rank_ref[first + m].astype(jnp.float32) + part

    def backward_chunk(slot, chunk, grads_rows):
        base = chunk * chunk_rows
        hid_grad = jnp.dot(
            grads_rows[base : base + chunk_rows], w_out_t_ref[...], preferred_element_type=jnp.float32
        )
        total = jnp.zeros((8, width), jnp.float32)
        for sub in range(0, chunk_rows, SUB_ROWS):
            place = pl.ds(base + sub, SUB_ROWS)
            pre_grad = hid_grad[sub : sub + SUB_ROWS] * slope_buf[slot, place, :]
            pre_buf[place, :] = pre_grad.astype(jnp.bfloat16)
            total = total + jnp.sum(pre_grad.reshape(SUB_ROWS // 8, 8, width), axis=0)
        bias_acc[...] += total

    def run(do_forward, do_backward):
        late = step - LAG
        if do_backward:
            for copy in copies(late):
                copy.wait()
            late_slot = lax.rem(late, LAG + 1)
            grads = loss_part(late)
            grads_b = grads.astype(jnp.bfloat16)
            grads_rows = jnp.transpose(grads, (1, 0)).astype(jnp.bfloat16)
        slot = lax.rem(step, LAG + 1)
        for chunk in range(rows // chunk_rows):
            if do_backward:
                backward_chunk(late_slot, chunk, grads_rows)
            if do_forward:
                forward_chunk(step, slot, chunk)
        if do_forward:
            for copy in copies(step):
                copy.start()
        if do_backward:
            small_ref[0:nvars, :] += jnp.dot(
                grads_b, hid_buf[late_slot], preferred_element_type=jnp.float32
            )
            grad_ref[...] += lax.dot_general(
                late_ref[...].reshape(rows, in_width),
                pre_buf[...],
                (((0,), (0,)), ((), ())),
                preferred_element_type=jnp.float32,
            )

    @pl.when(step == 0)
    def _():
        barrier = pltpu.get_barrier_semaphore()
        for hop in range(1, groups):
            pl.semaphore_signal(
                barrier,
                inc=1,
                device_id={"member": lax.rem(me + hop, groups)},
                device_id_type=pl.DeviceIdType.MESH,
            )
        pl.semaphore_wait(barrier, groups - 1)
        grad_ref[...] = jnp.zeros_like(grad_ref)
        small_ref[...] = jnp.zeros_like(small_ref)
        bias_acc[...] = jnp.zeros_like(bias_acc)
        out_acc[...] = jnp.zeros_like(out_acc)

    @pl.when(step < LAG)
    def _():
        run(True, False)

    @pl.when(jnp.logical_and(step >= LAG, step < tiles))
    def _():
        run(True, True)

    @pl.when(step >= tiles)
    def _():
        run(False, True)

    @pl.when(step == tiles + LAG - 1)
    def _():
        small_ref[nvars : nvars + 8, :] = bias_acc[...]
        small_ref[nvars + 8 : 2 * nvars + 8, :] = jnp.broadcast_to(
            jnp.sum(out_acc[...], axis=1, keepdims=True), (nvars, width)
        )


def shards(
    latent,
    weight_in,
    bias_in,
    weight_out,
    bias_out,
    member_rank,
    target_level,
    target_jitter,
    var_weight,
):
    mem_dev, cell_count, in_width = latent.shape
    width = weight_in.shape[1]
    nvars = weight_out.shape[1]
    groups = lax.axis_size("member")
    members = mem_dev * groups
    all_cells = cell_count * lax.axis_size("grid")
    loss_scale = 2.0 / math.sqrt(all_cells * members)
    tiles = cell_count // TILE
    rows = mem_dev * TILE
    first_cell = lax.axis_index("grid") * cell_count
    area = area_weights(first_cell, cell_count)
    weights = (var_weight[:, None] * area[None, :]) * loss_scale

    def now(step):
        return jnp.minimum(step, tiles - 1)

    def late(step):
        return jnp.maximum(step - LAG, 0)

    def whole(*shape):
        return pl.BlockSpec(shape, lambda step: (0,) * len(shape))

    cell_spec = pl.BlockSpec((nvars, TILE), lambda step: (0, late(step)))
    local_grad, small = pl.pallas_call(
        functools.partial(fused_kernel, groups, tiles),
        grid=(tiles + LAG,),
        in_specs=[
            pl.BlockSpec((mem_dev, TILE, in_width), lambda step: (0, now(step), 0)),
            pl.BlockSpec((mem_dev, TILE, in_width), lambda step: (0, late(step), 0)),
            whole(in_width, width),
            whole(1, width),
            whole(nvars, width),
            whole(nvars, 1),
            pl.BlockSpec((mem_dev, nvars, TILE), lambda step: (0, 0, now(step))),
            cell_spec,
            cell_spec,
            cell_spec,
        ],
        out_specs=[whole(in_width, width), whole(2 * nvars + 8, width)],
        out_shape=[
            jax.ShapeDtypeStruct((in_width, width), jnp.float32),
            jax.ShapeDtypeStruct((2 * nvars + 8, width), jnp.float32),
        ],
        scratch_shapes=[
            pltpu.VMEM((LAG + 1, rows, width), jnp.bfloat16),
            pltpu.VMEM((LAG + 1, rows, width), jnp.float32),
            pltpu.VMEM((rows, width), jnp.bfloat16),
            pltpu.VMEM((tiles, mem_dev * nvars, TILE), jnp.float32),
            pltpu.VMEM((tiles, mem_dev * nvars, TILE), jnp.float32),
            pltpu.VMEM((groups - 1, tiles, mem_dev * nvars, TILE), jnp.float32),
            pltpu.VMEM((8, width), jnp.float32),
            pltpu.VMEM((nvars, TILE), jnp.float32),
            pltpu.SemaphoreType.DMA((groups - 1, tiles)),
            pltpu.SemaphoreType.DMA((groups - 1, tiles)),
        ],
        compiler_params=pltpu.CompilerParams(
            collective_id=0,
            has_side_effects=True,
            vmem_limit_bytes=56 * 1024 * 1024,
            dimension_semantics=("arbitrary",),
        ),
    )(
        latent,
        latent,
        weight_in,
        bias_in.reshape(1, -1),
        weight_out.T,
        bias_out.reshape(-1, 1),
        member_rank,
        target_level,
        target_jitter,
        weights,
    )
    total = lax.psum(small, ("member", "grid"))
    grad_w_out = total[:nvars].T
    grad_b_in = jnp.sum(total[nvars : nvars + 8], axis=0)
    grad_b_out = total[nvars + 8 :, 0]
    summed = lax.psum(local_grad, "member")
    grad_shard = lax.psum_scatter(summed, "grid", scatter_dimension=0, tiled=True)
    return (grad_shard, grad_b_in, grad_w_out, grad_b_out)


def solution(mesh):
    in_specs = (
        P("member", "grid", None),
        P(),
        P(),
        P(),
        P(),
        P("member", None, "grid"),
        P(None, "grid"),
        P(None, "grid"),
        P(),
    )
    out_specs = (P("grid", None), P(), P(), P())
    return jax.shard_map(shards, mesh=mesh, in_specs=in_specs, out_specs=out_specs, check_vma=False)
```

```python
import functools
import math

import jax
import jax.numpy as jnp
from jax import lax
from jax.experimental import pallas as pl
from jax.experimental.pallas import tpu as pltpu
from jax.sharding import PartitionSpec as P

LONS = 1440
LAG = 2
TILE = 128
CHUNK_ROWS = 256
SUB_ROWS = 32

north_row = 200.0
mean_weight = 0.05
smooth_square = 0.01
root_two_pi = math.sqrt(2.0 / math.pi)
cube_coef = 0.044715


def area_weights(first_cell, count):
    global_cell = first_cell + jnp.arange(count, dtype=jnp.int32)
    lat_row = (global_cell // LONS).astype(jnp.float32)
    latitude = (90.0 - 0.25 * (north_row + lat_row)) * (math.pi / 180.0)
    return jnp.cos(latitude)


def soft_sign(values):
    return values * lax.rsqrt(values * values + smooth_square)


def fused_kernel(
    groups,
    tiles,
    lat_ref,
    late_ref,
    w_in_ref,
    b_in_ref,
    w_out_t_ref,
    b_out_ref,
    rank_ref,
    level_ref,
    jitter_ref,
    weight_ref,
    grad_ref,
    small_ref,
    hid_buf,
    slope_buf,
    pre_buf,
    field_buf,
    squash_buf,
    recv_buf,
    bias_acc,
    out_acc,
    send_sem,
    recv_sem,
    grad_acc,
    small_acc,
    b_out_col,
    pair_grad_in,
    pair_small_in,
    pair_sum,
    group_grad,
    group_small,
    group_sum,
    chip_grad,
    chip_small,
    final_grad,
    final_small,
    red_send,
    red_recv,
):
    step = pl.program_id(0)
    grid_me = lax.axis_index("grid")
    core = lax.rem(grid_me, 2)
    chip = grid_me // 2
    chips = grad_acc.shape[0]
    block_rows = grad_acc.shape[2]
    row_parts = min(groups, block_rows // 8)
    col_parts = groups // row_parts
    part_rows = block_rows // row_parts
    part_cols = grad_acc.shape[3] // col_parts
    me = lax.axis_index("member")
    mem_dev, tile, in_width = lat_ref.shape
    width = w_in_ref.shape[1]
    nvars = w_out_t_ref.shape[0]
    rows = mem_dev * tile
    members = mem_dev * groups
    mem_chunk = max(1, CHUNK_ROWS // tile)
    chunk_rows = mem_chunk * tile

    def copies(index):
        made = []
        for hop in range(1, groups):
            made.append(
                pltpu.make_async_remote_copy(
                    src_ref=field_buf.at[index],
                    dst_ref=recv_buf.at[hop - 1, index],
                    send_sem=send_sem.at[hop - 1, index],
                    recv_sem=recv_sem.at[hop - 1, index],
                    device_id={"member": lax.rem(me + hop, groups)},
                    device_id_type=pl.DeviceIdType.MESH,
                )
            )
        return made

    def loss_part(index):
        own = [field_buf[index, pl.ds(m * nvars, nvars), :] for m in range(mem_dev)]
        other = [
            recv_buf[g, index, pl.ds(m * nvars, nvars), :]
            for g in range(groups - 1)
            for m in range(mem_dev)
        ]
        target = 0.1 * level_ref[...].astype(jnp.float32) + 0.5 * jitter_ref[...] - 0.5
        center = own[0]
        for value in own[1:] + other:
            center = center + value
        pull = (2.0 * mean_weight) * (center * (1.0 / members) - target)
        weight = weight_ref[...]
        pair = [jnp.zeros_like(target) for _ in range(mem_dev)]
        for a in range(mem_dev):
            for b in range(a + 1, mem_dev):
                value = soft_sign(own[a] - own[b])
                pair[a] = pair[a] + value
                pair[b] = pair[b] - value
            for value in other:
                pair[a] = pair[a] + soft_sign(own[a] - value)
        grads = []
        for m in range(mem_dev):
            squash = squash_buf[index, pl.ds(m * nvars, nvars), :]
            slope = weight * (soft_sign(own[m] - target) - pair[m] * (1.0 / (members - 1)) + pull)
            grads.append(slope * (1.0 - squash * squash))
        total = grads[0]
        for value in grads[1:]:
            total = total + value
        out_acc[...] += total
        return jnp.concatenate(grads, axis=1)

    def forward_chunk(index, slot, chunk):
        first = chunk * mem_chunk
        block = lat_ref[pl.ds(first, mem_chunk)].reshape(chunk_rows, in_width)
        raw = jnp.dot(block, w_in_ref[...], preferred_element_type=jnp.float32)
        bias = b_in_ref[...]
        for sub in range(0, chunk_rows, SUB_ROWS):
            pre = raw[sub : sub + SUB_ROWS] + bias
            square = pre * pre
            arg = pre * (root_two_pi + (root_two_pi * cube_coef) * square)
            gate = 0.5 + 0.5 * jnp.tanh(arg)
            hid = pre * gate
            rate = (2.0 * root_two_pi) + (6.0 * root_two_pi * cube_coef) * square
            place = pl.ds(chunk * chunk_rows + sub, SUB_ROWS)
            hid_buf[slot, place, :] = hid.astype(jnp.bfloat16)
            slope_buf[slot, place, :] = gate + hid * (1.0 - gate) * rate
        hid_block = hid_buf[slot, pl.ds(chunk * chunk_rows, chunk_rows), :]
        outs = lax.dot_general(
            w_out_t_ref[...], hid_block, (((1,), (1,)), ((), ())), preferred_element_type=jnp.float32
        )
        squash = jnp.tanh(outs + jnp.tile(b_out_col[...], (1, chunk_rows // 128)))
        for m in range(mem_chunk):
            part = squash[:, m * tile : (m + 1) * tile]
            place = pl.ds((first + m) * nvars, nvars)
            squash_buf[index, place, :] = part
            field_buf[index, place, :] = 0.1 * rank_ref[first + m].astype(jnp.float32) + part

    def backward_chunk(slot, chunk, grads_rows):
        base = chunk * chunk_rows
        hid_grad = jnp.dot(
            grads_rows[base : base + chunk_rows], w_out_t_ref[...], preferred_element_type=jnp.float32
        )
        total = jnp.zeros((8, width), jnp.float32)
        for sub in range(0, chunk_rows, SUB_ROWS):
            place = pl.ds(base + sub, SUB_ROWS)
            pre_grad = hid_grad[sub : sub + SUB_ROWS] * slope_buf[slot, place, :]
            pre_buf[place, :] = pre_grad.astype(jnp.bfloat16)
            total = total + jnp.sum(pre_grad.reshape(SUB_ROWS // 8, 8, width), axis=0)
        bias_acc[...] += total

    def run(do_forward, do_backward):
        late = step - LAG
        if do_backward:
            for copy in copies(late):
                copy.wait()
            late_slot = lax.rem(late, LAG + 1)
            grads = loss_part(late)
            grads_b = grads.astype(jnp.bfloat16)
            grads_rows = jnp.transpose(grads, (1, 0)).astype(jnp.bfloat16)
        slot = lax.rem(step, LAG + 1)
        for chunk in range(rows // chunk_rows):
            if do_backward:
                backward_chunk(late_slot, chunk, grads_rows)
            if do_forward:
                forward_chunk(step, slot, chunk)
        if do_forward:
            for copy in copies(step):
                copy.start()
        if do_backward:
            small_acc[0] += jnp.dot(
                grads_b, hid_buf[late_slot], preferred_element_type=jnp.float32
            )
            grad_acc[...] += lax.dot_general(
                late_ref[...].reshape(rows, in_width),
                pre_buf[...],
                (((0,), (0,)), ((), ())),
                preferred_element_type=jnp.float32,
            ).reshape(grad_acc.shape)

    def member_id(hop):
        return {"member": lax.rem(me + hop, groups)}

    def core_id():
        return {"grid": chip * 2 + 1 - core}

    def chip_id(hop):
        return {"grid": lax.rem(chip + hop, chips) * 2 + core}

    def send(number, source, target, device):
        copy = pltpu.make_async_remote_copy(
            src_ref=source,
            dst_ref=target,
            send_sem=red_send.at[number],
            recv_sem=red_recv.at[number],
            device_id=device,
            device_id_type=pl.DeviceIdType.MESH,
        )
        copy.start()
        return copy

    def part_of(member):
        first_row = pl.multiple_of(lax.rem(member, row_parts) * part_rows, part_rows)
        first_col = pl.multiple_of((member // row_parts) * part_cols, part_cols)
        return pl.ds(first_row, part_rows), pl.ds(first_col, part_cols)

    def reduce_gradients():
        number = 0
        waits = [
            send(0, small_acc.at[1 - core], pair_small_in, core_id()),
            send(1, grad_acc.at[:, 1 - core], pair_grad_in, core_id()),
        ]
        number = 2
        for copy in waits:
            copy.wait()
        pair_sum[...] = grad_acc[:, core] + pair_grad_in[...]
        group_small[0] = small_acc[core] + pair_small_in[...]
        waits = []
        for hop in range(1, groups):
            rows_at, cols_at = part_of(lax.rem(me + hop, groups))
            waits.append(send(number, group_small.at[0], group_small.at[hop], member_id(hop)))
            waits.append(
                send(number + 1, pair_sum.at[:, rows_at, cols_at], group_grad.at[hop], member_id(hop))
            )
            number += 2
        rows_at, cols_at = part_of(me)
        group_grad[0] = pair_sum[:, rows_at, cols_at]
        for copy in waits:
            copy.wait()

        def in_order(ref, own, count):
            total = ref[own]
            for index in range(1, count):
                total = total + ref[lax.rem(own - index + count, count)]
            return total

        group_sum[...] = in_order(group_grad, me, groups)
        chip_small[0] = in_order(group_small, me, groups)
        chip_grad[0] = group_sum[chip]
        waits = []
        for hop in range(1, chips):
            target = lax.rem(chip + hop, chips)
            waits.append(send(number, group_sum.at[target], chip_grad.at[hop], chip_id(hop)))
            waits.append(send(number + 1, chip_small.at[0], chip_small.at[hop], chip_id(hop)))
            number += 2
        for copy in waits:
            copy.wait()
        final_grad[rows_at, cols_at] = in_order(chip_grad, chip, chips)
        final_small[core] = in_order(chip_small, chip, chips)
        waits = [send(number, final_small.at[core], final_small.at[core], core_id())]
        number += 1
        for hop in range(1, groups):
            piece = final_grad.at[rows_at, cols_at]
            waits.append(send(number, piece, piece, member_id(hop)))
            number += 1
        for copy in waits:
            copy.wait()
        grad_ref[...] = final_grad[...]
        small_ref[...] = final_small[...].reshape(small_ref.shape)

    @pl.when(step == 0)
    def _():
        barrier = pltpu.get_barrier_semaphore()
        peers = [member_id(hop) for hop in range(1, groups)] + [core_id()]
        peers += [chip_id(hop) for hop in range(1, chips)]
        for peer in peers:
            pl.semaphore_signal(barrier, inc=1, device_id=peer, device_id_type=pl.DeviceIdType.MESH)
        pl.semaphore_wait(barrier, len(peers))
        variable = lax.broadcasted_iota(jnp.int32, b_out_col.shape, 0)
        column = jnp.zeros(b_out_col.shape, jnp.float32)
        for index in range(nvars):
            column = jnp.where(variable == index, b_out_ref[index], column)
        b_out_col[...] = column
        grad_acc[...] = jnp.zeros_like(grad_acc)
        small_acc[...] = jnp.zeros_like(small_acc)
        bias_acc[...] = jnp.zeros_like(bias_acc)
        out_acc[...] = jnp.zeros_like(out_acc)

    @pl.when(step < LAG)
    def _():
        run(True, False)

    @pl.when(jnp.logical_and(step >= LAG, step < tiles))
    def _():
        run(True, True)

    @pl.when(step >= tiles)
    def _():
        run(False, True)

    @pl.when(step == tiles + LAG - 1)
    def _():
        sums = jnp.sum(out_acc[...], axis=1, keepdims=True)
        line = lax.broadcasted_iota(jnp.int32, (nvars, width), 0)
        lane = lax.broadcasted_iota(jnp.int32, (nvars, width), 1)
        spread = jnp.sum(jnp.where(line == lane, sums, 0.0), axis=0, keepdims=True)
        bias = jnp.sum(bias_acc[...], axis=0, keepdims=True)
        small_acc[1] = jnp.where(line == 0, bias, jnp.where(line == 1, spread, 0.0))
        reduce_gradients()


def shards(
    latent,
    weight_in,
    bias_in,
    weight_out,
    bias_out,
    member_rank,
    target_level,
    target_jitter,
    var_weight,
):
    mem_dev, cell_count, in_width = latent.shape
    width = weight_in.shape[1]
    nvars = weight_out.shape[1]
    groups = lax.axis_size("member")
    members = mem_dev * groups
    all_cells = cell_count * lax.axis_size("grid")
    loss_scale = 2.0 / math.sqrt(all_cells * members)
    tiles = cell_count // TILE
    rows = mem_dev * TILE
    shards_grid = lax.axis_size("grid")
    chips = shards_grid // 2
    block_rows = in_width // shards_grid
    row_parts = min(groups, block_rows // 8)
    part_rows = block_rows // row_parts
    part_cols = width // (groups // row_parts)
    copies = 3 + 3 * (groups - 1) + 2 * (chips - 1)
    first_cell = lax.axis_index("grid") * cell_count
    area = area_weights(first_cell, cell_count)
    weights = (var_weight[:, None] * area[None, :]) * loss_scale

    def now(step):
        return jnp.minimum(step, tiles - 1)

    def late(step):
        return jnp.maximum(step - LAG, 0)

    def whole(*shape):
        return pl.BlockSpec(shape, lambda step: (0,) * len(shape))

    cell_spec = pl.BlockSpec((nvars, TILE), lambda step: (0, late(step)))
    grad_shard, small = pl.pallas_call(
        functools.partial(fused_kernel, groups, tiles),
        grid=(tiles + LAG,),
        in_specs=[
            pl.BlockSpec((mem_dev, TILE, in_width), lambda step: (0, now(step), 0)),
            pl.BlockSpec((mem_dev, TILE, in_width), lambda step: (0, late(step), 0)),
            whole(in_width, width),
            whole(1, width),
            whole(nvars, width),
            pl.BlockSpec(memory_space=pltpu.SMEM),
            pl.BlockSpec((mem_dev, nvars, TILE), lambda step: (0, 0, now(step))),
            cell_spec,
            cell_spec,
            cell_spec,
        ],
        out_specs=[whole(block_rows, width), whole(2 * nvars, width)],
        out_shape=[
            jax.ShapeDtypeStruct((block_rows, width), jnp.float32),
            jax.ShapeDtypeStruct((2 * nvars, width), jnp.float32),
        ],
        scratch_shapes=[
            pltpu.VMEM((LAG + 1, rows, width), jnp.bfloat16),
            pltpu.VMEM((LAG + 1, rows, width), jnp.float32),
            pltpu.VMEM((rows, width), jnp.bfloat16),
            pltpu.VMEM((tiles, mem_dev * nvars, TILE), jnp.float32),
            pltpu.VMEM((tiles, mem_dev * nvars, TILE), jnp.float32),
            pltpu.VMEM((groups - 1, tiles, mem_dev * nvars, TILE), jnp.float32),
            pltpu.VMEM((8, width), jnp.float32),
            pltpu.VMEM((nvars, TILE), jnp.float32),
            pltpu.SemaphoreType.DMA((groups - 1, tiles)),
            pltpu.SemaphoreType.DMA((groups - 1, tiles)),
            pltpu.VMEM((chips, 2, block_rows, width), jnp.float32),
            pltpu.VMEM((2, nvars, width), jnp.float32),
            pltpu.VMEM((nvars, 128), jnp.float32),
            pltpu.VMEM((chips, block_rows, width), jnp.float32),
            pltpu.VMEM((nvars, width), jnp.float32),
            pltpu.VMEM((chips, block_rows, width), jnp.float32),
            pltpu.VMEM((groups, chips, part_rows, part_cols), jnp.float32),
            pltpu.VMEM((groups, nvars, width), jnp.float32),
            pltpu.VMEM((chips, part_rows, part_cols), jnp.float32),
            pltpu.VMEM((chips, part_rows, part_cols), jnp.float32),
            pltpu.VMEM((chips, nvars, width), jnp.float32),
            pltpu.VMEM((block_rows, width), jnp.float32),
            pltpu.VMEM((2, nvars, width), jnp.float32),
            pltpu.SemaphoreType.DMA((copies,)),
            pltpu.SemaphoreType.DMA((copies,)),
        ],
        compiler_params=pltpu.CompilerParams(
            collective_id=0,
            has_side_effects=True,
            vmem_limit_bytes=56 * 1024 * 1024,
            dimension_semantics=("arbitrary",),
        ),
    )(
        latent,
        latent,
        weight_in,
        bias_in.reshape(1, -1),
        weight_out.T,
        bias_out,
        member_rank,
        target_level,
        target_jitter,
        weights,
    )
    grad_w_out = small[:nvars].T
    grad_b_in = small[nvars]
    grad_b_out = small[nvars + 1, :nvars]
    return (grad_shard, grad_b_in, grad_w_out, grad_b_out)


def solution(mesh):
    in_specs = (
        P("member", "grid", None),
        P(),
        P(),
        P(),
        P(),
        P("member", None, "grid"),
        P(None, "grid"),
        P(None, "grid"),
        P(),
    )
    out_specs = (P("grid", None), P(), P(), P())
    return jax.shard_map(shards, mesh=mesh, in_specs=in_specs, out_specs=out_specs, check_vma=False)
```

```python
import functools
import math

import jax
import jax.numpy as jnp
from jax import lax
from jax.experimental import pallas as pl
from jax.experimental.pallas import tpu as pltpu
from jax.sharding import PartitionSpec as P

LONS = 1440
LAG = 2
TILE = 256
CHUNK_ROWS = 512
SUB_ROWS = 32

north_row = 200.0
mean_weight = 0.05
smooth_square = 0.01
root_two_pi = math.sqrt(2.0 / math.pi)
cube_coef = 0.044715


def soft_sign(values):
    return values * lax.rsqrt(values * values + smooth_square)


def fused_kernel(
    groups,
    tiles,
    loss_scale,
    lat_ref,
    late_ref,
    w_in_ref,
    b_in_ref,
    w_out_t_ref,
    b_out_ref,
    rank_ref,
    level_ref,
    jitter_ref,
    weight_ref,
    grad_ref,
    small_ref,
    hid_buf,
    slope_buf,
    pre_buf,
    field_buf,
    squash_buf,
    recv_buf,
    bias_acc,
    out_acc,
    send_sem,
    recv_sem,
    grad_acc,
    small_acc,
    b_out_col,
    weight_col,
    pair_grad_in,
    pair_small_in,
    pair_sum,
    group_grad,
    group_small,
    group_sum,
    chip_grad,
    chip_small,
    final_grad,
    final_small,
    red_send,
    red_recv,
):
    step = pl.program_id(0)
    grid_me = lax.axis_index("grid")
    core = lax.rem(grid_me, 2)
    chip = grid_me // 2
    chips = grad_acc.shape[0]
    block_rows = grad_acc.shape[2]
    row_parts = min(groups, block_rows // 8)
    col_parts = groups // row_parts
    part_rows = block_rows // row_parts
    part_cols = grad_acc.shape[3] // col_parts
    me = lax.axis_index("member")
    mem_dev, tile, in_width = lat_ref.shape
    width = w_in_ref.shape[1]
    nvars = w_out_t_ref.shape[0]
    rows = mem_dev * tile
    members = mem_dev * groups
    mem_chunk = min(mem_dev, max(1, CHUNK_ROWS // tile))
    chunk_rows = mem_chunk * tile

    def copies(index):
        made = []
        for hop in range(1, groups):
            made.append(
                pltpu.make_async_remote_copy(
                    src_ref=field_buf.at[index],
                    dst_ref=recv_buf.at[hop - 1, index],
                    send_sem=send_sem.at[hop - 1, index],
                    recv_sem=recv_sem.at[hop - 1, index],
                    device_id={"member": lax.rem(me + hop, groups)},
                    device_id_type=pl.DeviceIdType.MESH,
                )
            )
        return made

    def loss_part(index):
        own = [field_buf[index, pl.ds(m * nvars, nvars), :] for m in range(mem_dev)]
        other = [
            recv_buf[g, index, pl.ds(m * nvars, nvars), :]
            for g in range(groups - 1)
            for m in range(mem_dev)
        ]
        target = 0.1 * level_ref[...].astype(jnp.float32) + 0.5 * jitter_ref[...] - 0.5
        center = own[0]
        for value in own[1:] + other:
            center = center + value
        pull = (2.0 * mean_weight) * (center * (1.0 / members) - target)
        cell = grid_me * (tiles * tile) + index * tile + lax.broadcasted_iota(jnp.int32, (nvars, tile), 1)
        lat_row = jnp.floor((cell.astype(jnp.float32) + 0.5) * (1.0 / LONS))
        latitude = (90.0 - 0.25 * (north_row + lat_row)) * (math.pi / 180.0)
        weight = jnp.cos(latitude) * jnp.tile(weight_col[...], (1, tile // 128))
        pair = [jnp.zeros_like(target) for _ in range(mem_dev)]
        for a in range(mem_dev):
            for b in range(a + 1, mem_dev):
                value = soft_sign(own[a] - own[b])
                pair[a] = pair[a] + value
                pair[b] = pair[b] - value
            for value in other:
                pair[a] = pair[a] + soft_sign(own[a] - value)
        grads = []
        for m in range(mem_dev):
            squash = squash_buf[index, pl.ds(m * nvars, nvars), :]
            slope = weight * (soft_sign(own[m] - target) - pair[m] * (1.0 / (members - 1)) + pull)
            grads.append(slope * (1.0 - squash * squash))
        total = grads[0]
        for value in grads[1:]:
            total = total + value
        out_acc[...] += total
        return jnp.concatenate(grads, axis=1)

    def forward_chunk(index, slot, chunk):
        first = chunk * mem_chunk
        block = lat_ref[pl.ds(first, mem_chunk)].reshape(chunk_rows, in_width)
        raw = jnp.dot(block, w_in_ref[...], preferred_element_type=jnp.float32)
        bias = b_in_ref[...]
        for sub in range(0, chunk_rows, SUB_ROWS):
            pre = raw[sub : sub + SUB_ROWS] + bias
            square = pre * pre
            arg = pre * (root_two_pi + (root_two_pi * cube_coef) * square)
            gate = 0.5 + 0.5 * jnp.tanh(arg)
            hid = pre * gate
            rate = (2.0 * root_two_pi) + (6.0 * root_two_pi * cube_coef) * square
            place = pl.ds(chunk * chunk_rows + sub, SUB_ROWS)
            hid_buf[slot, place, :] = hid.astype(jnp.bfloat16)
            slope_buf[slot, place, :] = gate + hid * (1.0 - gate) * rate
        hid_block = hid_buf[slot, pl.ds(chunk * chunk_rows, chunk_rows), :]
        outs = lax.dot_general(
            w_out_t_ref[...], hid_block, (((1,), (1,)), ((), ())), preferred_element_type=jnp.float32
        )
        squash = jnp.tanh(outs + jnp.tile(b_out_col[...], (1, chunk_rows // 128)))
        for m in range(mem_chunk):
            part = squash[:, m * tile : (m + 1) * tile]
            place = pl.ds((first + m) * nvars, nvars)
            squash_buf[index, place, :] = part
            field_buf[index, place, :] = 0.1 * rank_ref[first + m].astype(jnp.float32) + part

    def backward_chunk(slot, chunk, grads_rows):
        base = chunk * chunk_rows
        hid_grad = jnp.dot(
            grads_rows[base : base + chunk_rows], w_out_t_ref[...], preferred_element_type=jnp.float32
        )
        total = jnp.zeros((8, width), jnp.float32)
        for sub in range(0, chunk_rows, SUB_ROWS):
            place = pl.ds(base + sub, SUB_ROWS)
            pre_grad = hid_grad[sub : sub + SUB_ROWS] * slope_buf[slot, place, :]
            pre_buf[place, :] = pre_grad.astype(jnp.bfloat16)
            total = total + jnp.sum(pre_grad.reshape(SUB_ROWS // 8, 8, width), axis=0)
        bias_acc[...] += total

    def run(do_forward, do_backward):
        late = step - LAG
        if do_backward:
            for copy in copies(late):
                copy.wait()
            late_slot = lax.rem(late, LAG + 1)
            grads = loss_part(late)
            grads_b = grads.astype(jnp.bfloat16)
            grads_rows = jnp.transpose(grads, (1, 0)).astype(jnp.bfloat16)
        slot = lax.rem(step, LAG + 1)
        for chunk in range(rows // chunk_rows):
            if do_backward:
                backward_chunk(late_slot, chunk, grads_rows)
            if do_forward:
                forward_chunk(step, slot, chunk)
        if do_forward:
            for copy in copies(step):
                copy.start()
        if do_backward:
            small_acc[0] += jnp.dot(
                grads_b, hid_buf[late_slot], preferred_element_type=jnp.float32
            )
            grad_acc[...] += lax.dot_general(
                late_ref[...].reshape(rows, in_width),
                pre_buf[...],
                (((0,), (0,)), ((), ())),
                preferred_element_type=jnp.float32,
            ).reshape(grad_acc.shape)

    def member_id(hop):
        return {"member": lax.rem(me + hop, groups)}

    def core_id():
        return {"grid": chip * 2 + 1 - core}

    def chip_id(hop):
        return {"grid": lax.rem(chip + hop, chips) * 2 + core}

    def send(number, source, target, device):
        copy = pltpu.make_async_remote_copy(
            src_ref=source,
            dst_ref=target,
            send_sem=red_send.at[number],
            recv_sem=red_recv.at[number],
            device_id=device,
            device_id_type=pl.DeviceIdType.MESH,
        )
        copy.start()
        return copy

    def part_of(member):
        first_row = pl.multiple_of(lax.rem(member, row_parts) * part_rows, part_rows)
        first_col = pl.multiple_of((member // row_parts) * part_cols, part_cols)
        return pl.ds(first_row, part_rows), pl.ds(first_col, part_cols)

    def reduce_gradients():
        def in_order(read, own, count):
            total = read(own)
            for index in range(1, count):
                total = total + read(lax.rem(own - index + count, count))
            return total

        order = [lax.rem(chip + hop, chips) for hop in range(1, chips + 1)]
        rows_at, cols_at = part_of(me)
        small_pair = send(0, small_acc.at[1 - core], pair_small_in, core_id())
        pairs = [
            send(1 + at, grad_acc.at[block, 1 - core], pair_grad_in.at[block], core_id())
            for at, block in enumerate(order)
        ]
        number = 1 + chips
        small_pair.wait()
        group_small[0] = small_acc[core] + pair_small_in[...]
        small_group = []
        for hop in range(1, groups):
            small_group.append(send(number, group_small.at[0], group_small.at[hop], member_id(hop)))
            number += 1
        members_waits = []
        for at, block in enumerate(order):
            pairs[at].wait()
            pair_sum[block] = grad_acc[block, core] + pair_grad_in[block]
            waits = []
            for hop in range(1, groups):
                rows_to, cols_to = part_of(lax.rem(me + hop, groups))
                piece = pair_sum.at[block, rows_to, cols_to]
                waits.append(send(number, piece, group_grad.at[hop, block], member_id(hop)))
                number += 1
            group_grad[0, block] = pair_sum[block, rows_at, cols_at]
            members_waits.append(waits)
        for copy in small_group:
            copy.wait()
        chip_small[0] = in_order(lambda slot: group_small[slot], me, groups)
        chip_waits = []
        for hop in range(1, chips):
            chip_waits.append(send(number, chip_small.at[0], chip_small.at[hop], chip_id(hop)))
            number += 1
        for at, block in enumerate(order):
            for copy in members_waits[at]:
                copy.wait()
            group_sum[block] = in_order(lambda slot: group_grad[slot, block], me, groups)
            if at < chips - 1:
                chip_waits.append(
                    send(number, group_sum.at[block], chip_grad.at[at + 1], chip_id(at + 1))
                )
                number += 1
            else:
                chip_grad[0] = group_sum[block]
        for copy in chip_waits:
            copy.wait()
        final_grad[rows_at, cols_at] = in_order(lambda slot: chip_grad[slot], chip, chips)
        final_small[core] = in_order(lambda slot: chip_small[slot], chip, chips)
        waits = [send(number, final_small.at[core], final_small.at[core], core_id())]
        number += 1
        for hop in range(1, groups):
            piece = final_grad.at[rows_at, cols_at]
            waits.append(send(number, piece, piece, member_id(hop)))
            number += 1
        for copy in waits:
            copy.wait()
        grad_ref[...] = final_grad[...]
        small_ref[...] = final_small[...].reshape(small_ref.shape)

    @pl.when(step == 0)
    def _():
        barrier = pltpu.get_barrier_semaphore()
        peers = [member_id(hop) for hop in range(1, groups)] + [core_id()]
        peers += [chip_id(hop) for hop in range(1, chips)]
        for peer in peers:
            pl.semaphore_signal(barrier, inc=1, device_id=peer, device_id_type=pl.DeviceIdType.MESH)
        pl.semaphore_wait(barrier, len(peers))
        variable = lax.broadcasted_iota(jnp.int32, b_out_col.shape, 0)
        column = jnp.zeros(b_out_col.shape, jnp.float32)
        for index in range(nvars):
            column = jnp.where(variable == index, b_out_ref[index], column)
        b_out_col[...] = column
        for index in range(nvars):
            column = jnp.where(variable == index, weight_ref[index] * loss_scale, column)
        weight_col[...] = column
        grad_acc[...] = jnp.zeros_like(grad_acc)
        small_acc[...] = jnp.zeros_like(small_acc)
        bias_acc[...] = jnp.zeros_like(bias_acc)
        out_acc[...] = jnp.zeros_like(out_acc)

    @pl.when(step < LAG)
    def _():
        run(True, False)

    @pl.when(jnp.logical_and(step >= LAG, step < tiles))
    def _():
        run(True, True)

    @pl.when(step >= tiles)
    def _():
        run(False, True)

    @pl.when(step == tiles + LAG - 1)
    def _():
        sums = jnp.sum(out_acc[...], axis=1, keepdims=True)
        line = lax.broadcasted_iota(jnp.int32, (nvars, width), 0)
        lane = lax.broadcasted_iota(jnp.int32, (nvars, width), 1)
        spread = jnp.sum(jnp.where(line == lane, sums, 0.0), axis=0, keepdims=True)
        bias = jnp.sum(bias_acc[...], axis=0, keepdims=True)
        small_acc[1] = jnp.where(line == 0, bias, jnp.where(line == 1, spread, 0.0))
        reduce_gradients()


def split_kernel(grad_ref, small_ref, grad_out, b_in_out, w_out_t_out, b_out_out):
    nvars = w_out_t_out.shape[0]
    grad_out[...] = grad_ref[...]
    w_out_t_out[...] = small_ref[0:nvars, :]
    b_in_out[...] = small_ref[nvars : nvars + 1, :]
    b_out_out[...] = small_ref[nvars + 1 : nvars + 2, 0:nvars]


def shards(
    latent,
    weight_in,
    bias_in,
    weight_out,
    bias_out,
    member_rank,
    target_level,
    target_jitter,
    var_weight,
):
    mem_dev, cell_count, in_width = latent.shape
    width = weight_in.shape[1]
    nvars = weight_out.shape[1]
    groups = lax.axis_size("member")
    members = mem_dev * groups
    all_cells = cell_count * lax.axis_size("grid")
    loss_scale = 2.0 / math.sqrt(all_cells * members)
    tiles = cell_count // TILE
    rows = mem_dev * TILE
    shards_grid = lax.axis_size("grid")
    chips = shards_grid // 2
    block_rows = in_width // shards_grid
    row_parts = min(groups, block_rows // 8)
    part_rows = block_rows // row_parts
    part_cols = width // (groups // row_parts)
    copies = chips * (groups + 2) + 2 * groups

    def now(step):
        return jnp.minimum(step, tiles - 1)

    def late(step):
        return jnp.maximum(step - LAG, 0)

    def whole(*shape):
        return pl.BlockSpec(shape, lambda step: (0,) * len(shape))

    cell_spec = pl.BlockSpec((nvars, TILE), lambda step: (0, late(step)))
    grad_shard, small = pl.pallas_call(
        functools.partial(fused_kernel, groups, tiles, loss_scale),
        grid=(tiles + LAG,),
        in_specs=[
            pl.BlockSpec((mem_dev, TILE, in_width), lambda step: (0, now(step), 0)),
            pl.BlockSpec((mem_dev, TILE, in_width), lambda step: (0, late(step), 0)),
            whole(in_width, width),
            whole(1, width),
            whole(nvars, width),
            pl.BlockSpec(memory_space=pltpu.SMEM),
            pl.BlockSpec((mem_dev, nvars, TILE), lambda step: (0, 0, now(step))),
            cell_spec,
            cell_spec,
            pl.BlockSpec(memory_space=pltpu.SMEM),
        ],
        out_specs=[whole(block_rows, width), whole(2 * nvars, width)],
        out_shape=[
            jax.ShapeDtypeStruct((block_rows, width), jnp.float32),
            jax.ShapeDtypeStruct((2 * nvars, width), jnp.float32),
        ],
        scratch_shapes=[
            pltpu.VMEM((LAG + 1, rows, width), jnp.bfloat16),
            pltpu.VMEM((LAG + 1, rows, width), jnp.float32),
            pltpu.VMEM((rows, width), jnp.bfloat16),
            pltpu.VMEM((tiles, mem_dev * nvars, TILE), jnp.float32),
            pltpu.VMEM((tiles, mem_dev * nvars, TILE), jnp.float32),
            pltpu.VMEM((groups - 1, tiles, mem_dev * nvars, TILE), jnp.float32),
            pltpu.VMEM((8, width), jnp.float32),
            pltpu.VMEM((nvars, TILE), jnp.float32),
            pltpu.SemaphoreType.DMA((groups - 1, tiles)),
            pltpu.SemaphoreType.DMA((groups - 1, tiles)),
            pltpu.VMEM((chips, 2, block_rows, width), jnp.float32),
            pltpu.VMEM((2, nvars, width), jnp.float32),
            pltpu.VMEM((nvars, 128), jnp.float32),
            pltpu.VMEM((nvars, 128), jnp.float32),
            pltpu.VMEM((chips, block_rows, width), jnp.float32),
            pltpu.VMEM((nvars, width), jnp.float32),
            pltpu.VMEM((chips, block_rows, width), jnp.float32),
            pltpu.VMEM((groups, chips, part_rows, part_cols), jnp.float32),
            pltpu.VMEM((groups, nvars, width), jnp.float32),
            pltpu.VMEM((chips, part_rows, part_cols), jnp.float32),
            pltpu.VMEM((chips, part_rows, part_cols), jnp.float32),
            pltpu.VMEM((chips, nvars, width), jnp.float32),
            pltpu.VMEM((block_rows, width), jnp.float32),
            pltpu.VMEM((2, nvars, width), jnp.float32),
            pltpu.SemaphoreType.DMA((copies,)),
            pltpu.SemaphoreType.DMA((copies,)),
        ],
        compiler_params=pltpu.CompilerParams(
            collective_id=0,
            has_side_effects=True,
            vmem_limit_bytes=56 * 1024 * 1024,
            dimension_semantics=("arbitrary",),
        ),
    )(
        latent,
        latent,
        weight_in,
        bias_in.reshape(1, -1),
        weight_out.T,
        bias_out,
        member_rank,
        target_level,
        target_jitter,
        var_weight,
    )
    grad_shard, grad_b_in, grad_w_out_t, grad_b_out = pl.pallas_call(
        split_kernel,
        out_shape=[
            jax.ShapeDtypeStruct((block_rows, width), jnp.float32),
            jax.ShapeDtypeStruct((1, width), jnp.float32),
            jax.ShapeDtypeStruct((nvars, width), jnp.float32),
            jax.ShapeDtypeStruct((1, nvars), jnp.float32),
        ],
    )(grad_shard, small)
    grad_b_in = grad_b_in.reshape(width)
    grad_w_out = grad_w_out_t.T
    grad_b_out = grad_b_out.reshape(nvars)
    return (grad_shard, grad_b_in, grad_w_out, grad_b_out)


def solution(mesh):
    in_specs = (
        P("member", "grid", None),
        P(),
        P(),
        P(),
        P(),
        P("member", None, "grid"),
        P(None, "grid"),
        P(None, "grid"),
        P(),
    )
    out_specs = (P("grid", None), P(), P(), P())
    return jax.shard_map(shards, mesh=mesh, in_specs=in_specs, out_specs=out_specs, check_vma=False)
```
